32 devices in a mesh: groups: 2 (over x), node: 16 (over z, y, core).
Axes of the slice: x: 2, y: 2, z: 4, core: 2. Of those that a mesh axis runs over, the one named last changes fastest.
Arguments:
- features: bfloat16 [32768, 1024], P(('groups', 'node')), parts along dimension 0, may hold values from -6 to 6
- filter_gate_weight: bfloat16 [64, 64], replicated, may hold values from -0.75 to 0.75
- skip_weight: bfloat16 [32, 256], replicated, may hold values from -1 to 1
- mix_weight: bfloat16 [96, 32], replicated, may hold values from -0.625 to 0.625
- band_weight: bfloat16 [16384, 192], P('node'), may hold values from -0.4375 to 0.4375
- far_weight: bfloat16 [64, 15360], P(None, 'node'), may hold values from -0.75 to 0.75
- far_ptr: int32 [16, 17], P('node'), may hold values from 0 to 15, as said below
- far_col: int32 [16, 15], P('node'), may hold values from 0 to 31, as said below
- export_block: int32 [16, 2], replicated, may hold values from 0 to 15, as said below
Outputs:
- residual_output: bfloat16 [32768, 512], P(('groups', 'node')), parts along dimension 0
- skip_out: bfloat16 [32768, 4096], P(('groups', 'node')), parts along dimension 0
The draws below stay inside these ranges and needn't reach their ends.
There are 2 independent parts, one for each index of `groups`. The reference program is written for one: setup_inputs(seed, part) draws one part's arguments, and reference() takes and returns one part's arrays. A program takes and returns all parts, laid end to end along the dimension named above; an argument that names none is the same for every part. Nothing has to cross between parts.
Inputs may be any that keep to these rules, and one draw needn't show every extreme that they name: Each row of export_block holds 2 different local block numbers, each below 16. `far_ptr`: each row starts at 0 and never falls; its last entry is the number of used far-block slots of that device, and some device uses all 15. `far_col`: slots below far_ptr[d][16] name blocks of devices other than d, at most one slot for each other device; the other slots hold 0 and belong to no block row. The device that uses all slots reads entry 0 of device 0 and the last entry of the last device.
All inputs are finite; a program needn't handle non-finite values.
Results may differ from the reference program's by a relative error of at most 0.0052.
Values may be sent and summed in bfloat16 or wider, within the bound.
A program may use at most 128 MiB of HBM per device.

```python
import jax
import jax.numpy as jnp
from jax import lax

BLK = 64
BLK_DEV = 16
TOUT = 16
DILATION_STEP = 16
EXPORT = 2
CHANNEL_WIDTH = 32
S = 256
TIN = 32
NODES = 16384
FAR_CAP = 15
N_NODE = 16


def far_plan(key):
    peer_count = FAR_CAP + 1
    key_list = jax.random.split(jax.random.fold_in(key, 17), 7)
    exports = jax.vmap(lambda subkey: jax.random.permutation(subkey, BLK_DEV)[:EXPORT])(jax.random.split(key_list[0], peer_count)).astype(jnp.int32)
    count_left = jax.random.randint(key_list[1], (peer_count,), 0, FAR_CAP + 1)
    count_right = jax.random.randint(key_list[2], (peer_count,), 0, FAR_CAP + 1)
    counts = FAR_CAP - count_left * count_right // (2 * FAR_CAP)
    busiest = jax.random.randint(key_list[3], (), 1, peer_count - 1)
    owners = jnp.arange(peer_count, dtype=jnp.int32)
    counts = jnp.where(owners == busiest, FAR_CAP, counts)
    orders = jax.vmap(lambda subkey: jax.random.permutation(subkey, FAR_CAP))(jax.random.split(key_list[4], peer_count)).astype(jnp.int32)
    sources = orders + (orders >= owners[:, None]).astype(jnp.int32)
    slot_pick = jax.random.randint(key_list[5], (peer_count, FAR_CAP), 0, EXPORT)
    forced_pick = jnp.where(sources == 0, 0, EXPORT - 1)
    slot_pick = jnp.where((owners == busiest)[:, None], forced_pick, slot_pick)
    slot_ids = jnp.arange(FAR_CAP, dtype=jnp.int32)[None, :]
    in_use = slot_ids < counts[:, None]
    columns = jnp.where(in_use, sources * EXPORT + slot_pick, 0).astype(jnp.int32)
    row_ids = jax.random.randint(key_list[6], (peer_count, FAR_CAP), 0, BLK_DEV)
    row_ids = jnp.sort(jnp.where(in_use, row_ids, BLK_DEV), axis=1)
    limits = jnp.arange(BLK_DEV + 1, dtype=jnp.int32)
    pointers = jnp.sum((row_ids[:, None, :] < limits[None, :, None]).astype(jnp.int32), axis=2).astype(jnp.int32)
    return (exports, columns, pointers)


def draw_far_ptr(key, part):
    return far_plan(key)[2]


def draw_far_col(key, part):
    return far_plan(key)[1]


def draw_export_block(key, part):
    return far_plan(key)[0]


def block_scale(rng, extent, cuts, smallest, largest):
    def one(axis_at, blocks):
        steps = jax.random.uniform(jax.random.fold_in(jax.random.fold_in(rng, 6), axis_at), (blocks,), jnp.float32, smallest / len(cuts), largest / len(cuts))
        return jnp.repeat(jnp.exp(steps), extent[axis_at] // blocks).reshape((-1,) + (1,) * (len(extent) - axis_at - 1))

    gain = one(*cuts[0])
    for cut in cuts[1:]:
        gain = gain * one(*cut)
    return gain


def noise(stream_key, dims, spread, bound, shards=(), kind=jnp.bfloat16):
    array = jax.random.normal(stream_key, dims, jnp.float32) * spread
    if len(shards) > 0:
        array = block_scale(stream_key, dims, shards, -0.22, 0.18) * array
    return jnp.clip(array, min=-bound, max=bound).astype(kind)


def setup_inputs(seed: int = 0, part: int = 0) -> dict:
    keys = jax.random.split(jax.random.key(seed), 10)
    part_splits = jax.random.split(jax.random.fold_in(keys[9], part), 10)
    features = noise(part_splits[0], (NODES, TIN * CHANNEL_WIDTH), 1.0, 6.0, ((0, 16),))
    filter_gate_weight = noise(keys[1], (2 * CHANNEL_WIDTH, 2 * CHANNEL_WIDTH), (2 * CHANNEL_WIDTH) ** -0.5, 0.75)
    skip_weight = noise(keys[2], (CHANNEL_WIDTH, S), CHANNEL_WIDTH ** -0.5, 1.0)
    mix_weight = noise(keys[3], (3 * CHANNEL_WIDTH, CHANNEL_WIDTH), (3 * CHANNEL_WIDTH) ** -0.5, 0.625)
    band_weight = noise(keys[4], (NODES, 3 * BLK), (3 * BLK) ** -0.5, 0.4375, ((0, 16),))
    far_weight = noise(keys[5], (BLK, N_NODE * FAR_CAP * BLK), BLK ** -0.5, 0.75, ((1, 16),))
    far_ptr = draw_far_ptr(jax.random.fold_in(keys[9], 71), part)
    far_col = draw_far_col(jax.random.fold_in(keys[9], 71), part)
    export_block = draw_export_block(jax.random.fold_in(keys[9], 71), part)
    return dict(features=features, filter_gate_weight=filter_gate_weight, skip_weight=skip_weight, mix_weight=mix_weight, band_weight=band_weight, far_weight=far_weight, far_ptr=far_ptr, far_col=far_col, export_block=export_block)


def front_part(args):
    series_input, filter_gate_weight, skip_weight = args
    earlier = series_input[:, :TOUT].astype(jnp.float32)
    later_taps = series_input[:, DILATION_STEP:].astype(jnp.float32)
    preact = jnp.einsum('myv,vi->myi', earlier, filter_gate_weight[:CHANNEL_WIDTH].astype(jnp.float32))
    preact = preact + jnp.einsum('myv,vi->myi', later_taps, filter_gate_weight[CHANNEL_WIDTH:].astype(jnp.float32))
    hidden = (jnp.tanh(preact[..., :CHANNEL_WIDTH]) * jax.nn.sigmoid(preact[..., CHANNEL_WIDTH:])).astype(jnp.bfloat16)
    skip_rows = jnp.einsum('ntc,cs->nts', hidden.astype(jnp.float32), skip_weight.astype(jnp.float32))
    return hidden, skip_rows.astype(jnp.bfloat16)


def diffuse(field_blocks, band_weight, far_weight, far_ptr, far_col, export_block):
    block_total = field_blocks.shape[0]
    width = field_blocks.shape[2]
    zero_block = jnp.zeros((1, BLK, width), jnp.bfloat16)
    padded = jnp.concatenate([zero_block, field_blocks, zero_block], axis=0).astype(jnp.float32)
    band_blocks = band_weight.reshape(block_total, BLK, 3 * BLK).astype(jnp.float32)
    summed = jnp.zeros((block_total, BLK, width), jnp.float32)
    for shift_pos in range(3):
        summed = summed + jnp.einsum('rij,rjm->rim', band_blocks[:, :, shift_pos * BLK:(shift_pos + 1) * BLK], padded[shift_pos:shift_pos + block_total])
    device_count = far_ptr.shape[0]
    far_cap = far_col.shape[1]
    weights_all = far_weight.reshape(BLK, device_count, far_cap, BLK).transpose(1, 2, 0, 3)

    def per_device(args):
        weights, columns, pointers = args
        owners = columns // EXPORT
        entries = columns % EXPORT
        block_ids = export_block[owners, entries]
        global_blocks = (owners * BLK_DEV + block_ids).astype(jnp.int32)
        pieces = field_blocks[global_blocks].astype(jnp.float32)
        products = jnp.einsum('kij,kjm->kim', weights.astype(jnp.float32), pieces, precision=lax.Precision.HIGHEST)
        slot_ids = jnp.arange(far_cap, dtype=jnp.int32)
        assign = ((pointers[:-1, None] <= slot_ids[None, :]) & (slot_ids[None, :] < pointers[1:, None])).astype(jnp.float32)
        return jnp.einsum('rk,kim->rim', assign, products, precision=lax.Precision.HIGHEST)

    far_terms = lax.map(per_device, (weights_all, far_col, far_ptr))
    summed = summed + far_terms.reshape(block_total, BLK, width)
    return summed.astype(jnp.bfloat16)


def reference(features, filter_gate_weight, skip_weight, mix_weight, band_weight, far_weight, far_ptr, far_col, export_block):
    device_count = far_ptr.shape[0]
    node_local = BLK_DEV * BLK
    series_all = features.reshape(device_count, node_local, TIN, CHANNEL_WIDTH)
    hidden_all, skip_all = lax.map(lambda series_input: front_part((series_input, filter_gate_weight, skip_weight)), series_all)
    block_total = device_count * BLK_DEV
    hidden_blocks = hidden_all.reshape(block_total, BLK, TOUT * CHANNEL_WIDTH)
    hop_one = diffuse(hidden_blocks, band_weight, far_weight, far_ptr, far_col, export_block)
    hop_two = diffuse(hop_one, band_weight, far_weight, far_ptr, far_col, export_block)

    def mix_part(args):
        series_input, hidden, first_hop, second_hop = args
        joined = jnp.concatenate([hidden, first_hop.reshape(node_local, TOUT, CHANNEL_WIDTH), second_hop.reshape(node_local, TOUT, CHANNEL_WIDTH)], axis=-1)
        mixed_state = jnp.einsum('myv,vi->myi', joined.astype(jnp.float32), mix_weight.astype(jnp.float32))
        return (series_input[:, DILATION_STEP:].astype(jnp.float32) + mixed_state).astype(jnp.bfloat16)

    residual_all = lax.map(mix_part, (series_all, hidden_all, hop_one.reshape(device_count, node_local, TOUT * CHANNEL_WIDTH), hop_two.reshape(device_count, node_local, TOUT * CHANNEL_WIDTH)))
    residual_output = residual_all.reshape(device_count * node_local, TOUT * CHANNEL_WIDTH)
    skip_out = skip_all.reshape(device_count * node_local, TOUT * S)
    return residual_output, skip_out
```

```python
import functools

import jax
import jax.numpy as jnp
from jax import lax
from jax.experimental import pallas as pl
from jax.experimental.pallas import tpu as pltpu
from jax.sharding import PartitionSpec as P

BLK = 64
TOUT = 16
EXPORT = 2
CH = 32
S = 256
PARTS = 2
GROUP = 4
MESH = pl.DeviceIdType.MESH
BF16 = jnp.bfloat16
F32 = jnp.float32


def dot(a, b):
    return jnp.dot(a, b, preferred_element_type=F32)


def one_hot(shape, rule):
    row = lax.broadcasted_iota(jnp.int32, shape, 0)
    col = lax.broadcasted_iota(jnp.int32, shape, 1)
    return jnp.where(rule(row, col), 1.0, 0.0).astype(BF16)


def front_kernel(x_ref, fg_ref, skip_ref, hidden_ref, out_ref, fg_wide, skip_wide):
    lanes = 4 * CH

    @pl.when(pl.program_id(0) == 0)
    def _():
        rows = one_hot((lanes, CH), lambda r, c: r % CH == c)
        spread = one_hot((2 * CH, 2 * lanes), lambda r, c: r == c % CH + CH * (c // lanes))
        keep = one_hot((lanes, 2 * lanes), lambda r, c: r // CH == (c % lanes) // CH)
        for tap in range(2):
            tall = dot(rows, fg_ref[tap * CH : (tap + 1) * CH, :]).astype(BF16)
            fg_wide[tap * lanes : (tap + 1) * lanes, :] = dot(tall, spread).astype(BF16) * keep
        tall = dot(rows, skip_ref[...]).astype(BF16)
        for step in range(4):
            mine = one_hot((lanes, S), lambda r, c: r // CH == step)
            skip_wide[:, step * S : (step + 1) * S] = tall * mine

    for j in range(TOUT // 4):
        early = x_ref[:, j * lanes : (j + 1) * lanes]
        late = x_ref[:, TOUT * CH + j * lanes : TOUT * CH + (j + 1) * lanes]
        pre = dot(jnp.concatenate([early, late], axis=1), fg_wide[...])
        gate = 0.5 * jnp.tanh(0.5 * pre[:, lanes:]) + 0.5
        hidden = (jnp.tanh(pre[:, :lanes]) * gate).astype(BF16)
        hidden_ref[:, j * lanes : (j + 1) * lanes] = hidden
        out_ref[:, j * 4 * S : (j + 1) * 4 * S] = dot(hidden, skip_wide[...]).astype(BF16)


def front(features, fg, skip):
    rows = features.shape[0]
    tile = 128
    return pl.pallas_call(
        front_kernel,
        grid=(rows // tile,),
        in_specs=[
            pl.BlockSpec((tile, features.shape[1]), lambda i: (i, 0)),
            pl.BlockSpec(fg.shape, lambda i: (0, 0)),
            pl.BlockSpec(skip.shape, lambda i: (0, 0)),
        ],
        out_specs=[
            pl.BlockSpec((tile, TOUT * CH), lambda i: (i, 0)),
            pl.BlockSpec((tile, TOUT * S), lambda i: (i, 0)),
        ],
        out_shape=[
            jax.ShapeDtypeStruct((rows, TOUT * CH), BF16),
            jax.ShapeDtypeStruct((rows, TOUT * S), BF16),
        ],
        scratch_shapes=[pltpu.VMEM((8 * CH, 8 * CH), BF16), pltpu.VMEM((4 * CH, 4 * S), BF16)],
        compiler_params=pltpu.CompilerParams(vmem_limit_bytes=32 * 2**20),
        name="front",
    )(features, fg, skip)


def hops_kernel(
    n, zs, ys,
    hid, feat, band, farw, mix, ptr, col, exports,
    out,
    gat_0, gat_1, gat_2, gat_3, halo, fld, pieces, far_mat, band_mat, mix_wide, late, part,
    send_sem, recv_sem, halo_send, halo_recv, local_sem,
):
    rows = hid.shape[0]
    blocks = rows // BLK
    width = hid.shape[1] // PARTS
    slots = col.shape[1]
    gat = [[gat_0, gat_1], [gat_2, gat_3]]
    me = lax.axis_index("node")
    core = me % 2
    y = (me // 2) % ys
    z = me // (2 * ys)

    def index(a, b, c):
        return (a * ys + b) * 2 + c

    z_from = [lax.rem(z + zs - i, zs) for i in range(zs)]
    z_to = [lax.rem(z + i, zs) for i in range(zs)]
    other_y = ys - 1 - y
    across = index(z, other_y, core)
    mate = index(z, y, 1 - core)

    feat_copy = pltpu.make_async_copy(
        feat.at[:, TOUT * CH : 2 * TOUT * CH], late, local_sem.at[0]
    )
    feat_copy.start()

    barrier = pltpu.get_barrier_semaphore()
    greet = [index(z_to[i], y, core) for i in range(1, zs)] + [mate]
    greet += [lax.rem(me + 1, n), lax.rem(me + n - 1, n)]
    if ys > 1:
        greet.append(across)
    for peer in greet:
        pl.semaphore_signal(barrier, inc=1, device_id={"node": peer}, device_id_type=MESH)

    for h in range(PARTS):
        field = hid[:, h * width : (h + 1) * width]
        fld[0, h, 1 : blocks + 1] = field.reshape(blocks, BLK, width)

    def stage(p, h):
        for e in range(EXPORT):
            gat[p][h][me * EXPORT + e] = fld[p, h, exports[me, e] + 1]

    stage(0, 0)
    pl.semaphore_wait(barrier, len(greet))

    def chunk_copy(p, h, source, target, sem):
        return pltpu.make_async_remote_copy(
            src_ref=gat[p][h].at[pl.ds(source * EXPORT, EXPORT)],
            dst_ref=gat[p][h].at[pl.ds(source * EXPORT, EXPORT)],
            send_sem=send_sem.at[p, h, sem],
            recv_sem=recv_sem.at[p, h, source],
            device_id={"node": target},
            device_id_type=MESH,
        )

    def halo_copy(p, h, side, target):
        first = blocks if side == 0 else 1
        return pltpu.make_async_remote_copy(
            src_ref=fld.at[p, h, first],
            dst_ref=halo.at[p, h, side],
            send_sem=halo_send.at[p, h, side],
            recv_sem=halo_recv.at[p, h, side],
            device_id={"node": target},
            device_id_type=MESH,
        )

    y_sems = zs - 1
    mate_sems = y_sems + (zs if ys > 1 else 0)
    sends = []

    def go(p, h, source, target, sem):
        copy = chunk_copy(p, h, source, target, sem)
        copy.start()
        sends.append(copy)

    def arrived(p, h, source):
        chunk_copy(p, h, source, mate, 0).wait_recv()

    def start_own(p, h):
        for i in range(1, zs):
            go(p, h, me, index(z_to[i], y, core), i - 1)
        if ys > 1:
            go(p, h, me, across, y_sems)
        go(p, h, me, mate, mate_sems)

        @pl.when(me < n - 1)
        def _():
            halo_copy(p, h, 0, me + 1).start()

        @pl.when(me > 0)
        def _():
            halo_copy(p, h, 1, me - 1).start()

    def pass_z(p, h):
        for i in range(1, zs):
            source = index(z_from[i], y, core)
            arrived(p, h, source)
            if ys > 1:
                go(p, h, source, across, y_sems + i)
            go(p, h, source, mate, mate_sems + i)

    def pass_y(p, h):
        if ys > 1:
            for i in range(zs):
                source = index(z_from[i], other_y, core)
                arrived(p, h, source)
                go(p, h, source, mate, mate_sems + zs + i)

    def finish(p, h):
        for side_y in [y, other_y][:ys]:
            for i in range(zs):
                arrived(p, h, index(z_from[i], side_y, 1 - core))

        @pl.when(me > 0)
        def _():
            halo_copy(p, h, 0, me - 1).wait_recv()

        @pl.when(me < n - 1)
        def _():
            halo_copy(p, h, 1, me + 1).wait_recv()

        fld[p, h, 0] = halo[p, h, 0]
        fld[p, h, blocks + 1] = halo[p, h, 1]
        for k in range(slots):
            pieces[k * BLK : (k + 1) * BLK, :] = gat[p][h][col[0, k]]

    def diffuse(p, h, g):
        high = GROUP * BLK
        lines = slice(g * high, (g + 1) * high)
        field = fld[p, h, g * GROUP : (g + 1) * GROUP + 2].reshape(high + 2 * BLK, width)
        near = dot(band_mat[lines, :], field)
        return near + dot(far_mat[lines, :], pieces[...])

    def build():
        for r in range(blocks):
            i = r % GROUP
            shift = one_hot((3 * BLK, (GROUP + 2) * BLK), lambda a, b: a + i * BLK == b)
            lines = slice(r * BLK, (r + 1) * BLK)
            band_mat[lines, :] = dot(band[lines, :], shift).astype(BF16)
            slot = lax.broadcasted_iota(jnp.int32, (1, slots * BLK), 1) // BLK
            used = jnp.logical_and(slot >= ptr[0, r], slot < ptr[0, r + 1])
            far_mat[lines, :] = farw[...] * jnp.where(used, 1.0, 0.0).astype(BF16)
        size = mix_wide.shape[1]
        tall_rule = one_hot((size, CH), lambda a, b: a % CH == b)
        wide_rule = one_hot((CH, size), lambda a, b: a == b % CH)
        keep = one_hot((size, size), lambda a, b: a // CH == b // CH)
        for term in range(3):
            tall = dot(tall_rule, mix[term * CH : (term + 1) * CH, :]).astype(BF16)
            mix_wide[term] = dot(tall, wide_rule).astype(BF16) * keep

    def hop_one(h):
        for g in range(blocks // GROUP):
            field = diffuse(0, h, g).astype(BF16).reshape(GROUP, BLK, width)
            fld[1, h, 1 + g * GROUP : 1 + (g + 1) * GROUP] = field

    def mix_early(h):
        columns = slice(h * width, (h + 1) * width)
        part[:, columns] = (
            late[:, columns].astype(F32)
            + dot(fld[0, h, 1 : blocks + 1].reshape(rows, width), mix_wide[0])
            + dot(fld[1, h, 1 : blocks + 1].reshape(rows, width), mix_wide[1])
        )

    def hop_two(h):
        columns = slice(h * width, (h + 1) * width)
        for g in range(blocks // GROUP):
            lines = slice(g * GROUP * BLK, (g + 1) * GROUP * BLK)
            field = diffuse(1, h, g).astype(BF16)
            out[lines, columns] = (part[lines, columns] + dot(field, mix_wide[2])).astype(BF16)

    start_own(0, 0)
    stage(0, 1)
    start_own(0, 1)

    @pl.when(me == 0)
    def _():
        for p in range(2):
            for h in range(PARTS):
                halo[p, h, 0] = jnp.zeros((BLK, width), BF16)

    @pl.when(me == n - 1)
    def _():
        for p in range(2):
            for h in range(PARTS):
                halo[p, h, 1] = jnp.zeros((BLK, width), BF16)

    pass_z(0, 0)
    build()
    feat_copy.wait()
    pass_y(0, 0)
    pass_z(0, 1)
    finish(0, 0)
    hop_one(0)
    stage(1, 0)
    start_own(1, 0)
    pass_y(0, 1)
    pass_z(1, 0)
    finish(0, 1)
    hop_one(1)
    stage(1, 1)
    start_own(1, 1)
    mix_early(0)
    pass_y(1, 0)
    pass_z(1, 1)
    mix_early(1)
    finish(1, 0)
    hop_two(0)
    pass_y(1, 1)
    finish(1, 1)
    hop_two(1)
    for copy in sends:
        copy.wait_send()
    for p in range(2):
        for h in range(PARTS):

            @pl.when(me < n - 1)
            def _():
                halo_copy(p, h, 0, me + 1).wait_send()

            @pl.when(me > 0)
            def _():
                halo_copy(p, h, 1, me - 1).wait_send()


def hops(n, hidden, features, band, farw, mix, ptr, col, exports):
    rows, columns = hidden.shape
    ys = 2 if n == 16 else 1
    zs = n // (2 * ys)
    width = columns // PARTS
    chunk_sends = zs - 1 + (zs if ys > 1 else 0) + zs * ys
    vmem = pl.BlockSpec(memory_space=pltpu.VMEM)
    smem = pl.BlockSpec(memory_space=pltpu.SMEM)
    return pl.pallas_call(
        functools.partial(hops_kernel, n, zs, ys),
        in_specs=[vmem, pl.BlockSpec(memory_space=pl.ANY), vmem, vmem, vmem, smem, smem, smem],
        out_specs=vmem,
        out_shape=jax.ShapeDtypeStruct((rows, columns), BF16),
        scratch_shapes=[
            *[pltpu.VMEM((n * EXPORT, BLK, width), BF16)] * (2 * PARTS),
            pltpu.VMEM((2, PARTS, 2, BLK, width), BF16),
            pltpu.VMEM((2, PARTS, rows // BLK + 2, BLK, width), BF16),
            pltpu.VMEM((farw.shape[1], width), BF16),
            pltpu.VMEM((rows, farw.shape[1]), BF16),
            pltpu.VMEM((rows, (GROUP + 2) * BLK), BF16),
            pltpu.VMEM((3, width, width), BF16),
            pltpu.VMEM((rows, columns), BF16),
            pltpu.VMEM((rows, columns), F32),
            pltpu.SemaphoreType.DMA((2, PARTS, chunk_sends)),
            pltpu.SemaphoreType.DMA((2, PARTS, n)),
            pltpu.SemaphoreType.DMA((2, PARTS, 2)),
            pltpu.SemaphoreType.DMA((2, PARTS, 2)),
            pltpu.SemaphoreType.DMA((1,)),
        ],
        compiler_params=pltpu.CompilerParams(
            collective_id=0, has_side_effects=True, vmem_limit_bytes=52 * 2**20
        ),
        name="hops",
    )(hidden, features, band, farw, mix, ptr, col, exports)


def solution(mesh):
    n = mesh.shape["node"]

    def local(features, fg, skip, mix, band, farw, ptr, col, exports):
        hidden, skip_out = front(features, fg, skip)
        residual = hops(n, hidden, features, band, farw, mix, ptr, col, exports)
        return residual, skip_out

    rows = P(("groups", "node"), None)
    return jax.shard_map(
        local,
        mesh=mesh,
        in_specs=(
            rows, P(), P(), P(), P("node", None), P(None, "node"), P("node", None), P("node", None), P(),
        ),
        out_specs=(rows, rows),
        check_vma=False,
    )
```

```python
import functools

import jax
import jax.numpy as jnp
from jax import lax
from jax.experimental import pallas as pl
from jax.experimental.pallas import tpu as pltpu
from jax.sharding import PartitionSpec as P

BLK = 64
TOUT = 16
EXPORT = 2
CH = 32
S = 256
PARTS = 2
GROUP = 4
MESH = pl.DeviceIdType.MESH
BF16 = jnp.bfloat16
F32 = jnp.float32


def dot(a, b):
    return jnp.dot(a, b, preferred_element_type=F32)


def one_hot(shape, rule):
    row = lax.broadcasted_iota(jnp.int32, shape, 0)
    col = lax.broadcasted_iota(jnp.int32, shape, 1)
    return jnp.where(rule(row, col), 1.0, 0.0).astype(BF16)


def front_kernel(x_ref, fg_ref, skip_ref, hidden_ref, out_ref, fg_wide, skip_wide):
    lanes = 4 * CH

    @pl.when(pl.program_id(0) == 0)
    def _():
        rows = one_hot((lanes, CH), lambda r, c: r % CH == c)
        spread = one_hot((2 * CH, 2 * lanes), lambda r, c: r == c % CH + CH * (c // lanes))
        keep = one_hot((lanes, 2 * lanes), lambda r, c: r // CH == (c % lanes) // CH)
        for tap in range(2):
            tall = dot(rows, fg_ref[tap * CH : (tap + 1) * CH, :]).astype(BF16)
            fg_wide[tap * lanes : (tap + 1) * lanes, :] = dot(tall, spread).astype(BF16) * keep
        tall = dot(rows, skip_ref[...]).astype(BF16)
        for step in range(4):
            mine = one_hot((lanes, S), lambda r, c: r // CH == step)
            skip_wide[:, step * S : (step + 1) * S] = tall * mine

    for j in range(TOUT // 4):
        early = x_ref[:, j * lanes : (j + 1) * lanes]
        late = x_ref[:, TOUT * CH + j * lanes : TOUT * CH + (j + 1) * lanes]
        pre = dot(jnp.concatenate([early, late], axis=1), fg_wide[...])
        gate = 0.5 * jnp.tanh(0.5 * pre[:, lanes:]) + 0.5
        hidden = (jnp.tanh(pre[:, :lanes]) * gate).astype(BF16)
        hidden_ref[:, j * lanes : (j + 1) * lanes] = hidden
        out_ref[:, j * 4 * S : (j + 1) * 4 * S] = dot(hidden, skip_wide[...]).astype(BF16)


def front(features, fg, skip):
    rows = features.shape[0]
    tile = 128
    return pl.pallas_call(
        front_kernel,
        grid=(rows // tile,),
        in_specs=[
            pl.BlockSpec((tile, features.shape[1]), lambda i: (i, 0)),
            pl.BlockSpec(fg.shape, lambda i: (0, 0)),
            pl.BlockSpec(skip.shape, lambda i: (0, 0)),
        ],
        out_specs=[
            pl.BlockSpec((tile, TOUT * CH), lambda i: (i, 0)),
            pl.BlockSpec((tile, TOUT * S), lambda i: (i, 0)),
        ],
        out_shape=[
            jax.ShapeDtypeStruct((rows, TOUT * CH), BF16),
            jax.ShapeDtypeStruct((rows, TOUT * S), BF16),
        ],
        scratch_shapes=[pltpu.VMEM((8 * CH, 8 * CH), BF16), pltpu.VMEM((4 * CH, 4 * S), BF16)],
        compiler_params=pltpu.CompilerParams(vmem_limit_bytes=60 * 2**20),
        name="front",
    )(features, fg, skip)


def hops_kernel(
    n, zs, ys,
    hid, feat, band, farw, mix, ptr, col, exports,
    out,
    gat_0, gat_1, gat_2, gat_3, halo, fld, pieces, far_mat, band_mat, mix_wide, late, part,
    send_sem, recv_sem, halo_send, halo_recv, local_sem,
):
    rows = hid.shape[0]
    blocks = rows // BLK
    width = hid.shape[1] // PARTS
    slots = col.shape[1]
    gat = [[gat_0, gat_1], [gat_2, gat_3]]
    me = lax.axis_index("node")
    core = me % 2
    y = (me // 2) % ys
    z = me // (2 * ys)

    def index(a, b, c):
        return (a * ys + b) * 2 + c

    z_from = [lax.rem(z + zs - i, zs) for i in range(zs)]
    z_to = [lax.rem(z + i, zs) for i in range(zs)]
    other_y = ys - 1 - y
    across = index(z, other_y, core)
    mate = index(z, y, 1 - core)

    feat_copy = pltpu.make_async_copy(
        feat.at[:, TOUT * CH : 2 * TOUT * CH], late, local_sem.at[0]
    )
    feat_copy.start()

    barrier = pltpu.get_barrier_semaphore()
    greet = [index(z_to[i], y, core) for i in range(1, zs)] + [mate]
    greet += [lax.rem(me + 1, n), lax.rem(me + n - 1, n)]
    if ys > 1:
        greet.append(across)
    for peer in greet:
        pl.semaphore_signal(barrier, inc=1, device_id={"node": peer}, device_id_type=MESH)

    for h in range(PARTS):
        field = hid[:, h * width : (h + 1) * width]
        fld[0, h, 1 : blocks + 1] = field.reshape(blocks, BLK, width)

    def stage(p, h):
        for e in range(EXPORT):
            gat[p][h][me * EXPORT + e] = fld[p, h, exports[e, me] + 1]

    stage(0, 0)
    pl.semaphore_wait(barrier, len(greet))

    def chunk_copy(p, h, source, target, sem):
        return pltpu.make_async_remote_copy(
            src_ref=gat[p][h].at[pl.ds(source * EXPORT, EXPORT)],
            dst_ref=gat[p][h].at[pl.ds(source * EXPORT, EXPORT)],
            send_sem=send_sem.at[p, h, sem],
            recv_sem=recv_sem.at[p, h, source],
            device_id={"node": target},
            device_id_type=MESH,
        )

    def halo_copy(p, h, side, target):
        first = blocks if side == 0 else 1
        return pltpu.make_async_remote_copy(
            src_ref=fld.at[p, h, first],
            dst_ref=halo.at[p, h, side],
            send_sem=halo_send.at[p, h, side],
            recv_sem=halo_recv.at[p, h, side],
            device_id={"node": target},
            device_id_type=MESH,
        )

    y_sems = zs - 1
    mate_sems = y_sems + (zs if ys > 1 else 0)
    sends = []

    def go(p, h, source, target, sem):
        copy = chunk_copy(p, h, source, target, sem)
        copy.start()
        sends.append(copy)

    def arrived(p, h, source):
        chunk_copy(p, h, source, mate, 0).wait_recv()

    def start_own(p, h):
        for i in range(1, zs):
            go(p, h, me, index(z_to[i], y, core), i - 1)
        if ys > 1:
            go(p, h, me, across, y_sems)
        go(p, h, me, mate, mate_sems)

        @pl.when(me < n - 1)
        def _():
            halo_copy(p, h, 0, me + 1).start()

        @pl.when(me > 0)
        def _():
            halo_copy(p, h, 1, me - 1).start()

    def pass_z(p, h):
        for i in range(1, zs):
            source = index(z_from[i], y, core)
            arrived(p, h, source)
            if ys > 1:
                go(p, h, source, across, y_sems + i)
            go(p, h, source, mate, mate_sems + i)

    def pass_y(p, h):
        if ys > 1:
            for i in range(zs):
                source = index(z_from[i], other_y, core)
                arrived(p, h, source)
                go(p, h, source, mate, mate_sems + zs + i)

    def finish(p, h):
        for side_y in [y, other_y][:ys]:
            for i in range(zs):
                arrived(p, h, index(z_from[i], side_y, 1 - core))

        @pl.when(me > 0)
        def _():
            halo_copy(p, h, 0, me - 1).wait_recv()

        @pl.when(me < n - 1)
        def _():
            halo_copy(p, h, 1, me + 1).wait_recv()

        fld[p, h, 0] = halo[p, h, 0]
        fld[p, h, blocks + 1] = halo[p, h, 1]
        for k in range(slots):
            pieces[k * BLK : (k + 1) * BLK, :] = gat[p][h][col[0, k]]

    def diffuse(p, h, g):
        high = GROUP * BLK
        lines = slice(g * high, (g + 1) * high)
        field = fld[p, h, g * GROUP : (g + 1) * GROUP + 2].reshape(high + 2 * BLK, width)
        near = dot(band_mat[lines, :], field)
        return near + dot(far_mat[lines, :], pieces[...])

    def build():
        for r in range(blocks):
            i = r % GROUP
            lines = slice(r * BLK, (r + 1) * BLK)
            if i == 0:
                high = jnp.transpose(band[:, r * BLK : (r + GROUP) * BLK])
            shift = one_hot((3 * BLK, (GROUP + 2) * BLK), lambda a, b: a + i * BLK == b)
            band_mat[lines, :] = dot(high[i * BLK : (i + 1) * BLK, :], shift).astype(BF16)
            slot = lax.broadcasted_iota(jnp.int32, (1, slots * BLK), 1) // BLK
            used = jnp.logical_and(slot >= ptr[0, r], slot < ptr[0, r + 1])
            far_mat[lines, :] = farw[...] * jnp.where(used, 1.0, 0.0).astype(BF16)
        size = mix_wide.shape[1]
        wide_rule = one_hot((CH, size), lambda a, b: a == b % CH)
        keep = one_hot((size, size), lambda a, b: a // CH == b // CH)
        for term in range(3):
            rule = one_hot((size, 3 * CH), lambda a, b: a % CH + term * CH == b)
            tall = lax.dot_general(
                rule, mix[...], (((1,), (1,)), ((), ())), preferred_element_type=F32
            ).astype(BF16)
            mix_wide[term] = dot(tall, wide_rule).astype(BF16) * keep

    def hop_one(h):
        for g in range(blocks // GROUP):
            field = diffuse(0, h, g).astype(BF16).reshape(GROUP, BLK, width)
            fld[1, h, 1 + g * GROUP : 1 + (g + 1) * GROUP] = field

    def mix_early(h):
        columns = slice(h * width, (h + 1) * width)
        part[:, columns] = (
            late[:, columns].astype(F32)
            + dot(fld[0, h, 1 : blocks + 1].reshape(rows, width), mix_wide[0])
            + dot(fld[1, h, 1 : blocks + 1].reshape(rows, width), mix_wide[1])
        )

    def hop_two(h):
        columns = slice(h * width, (h + 1) * width)
        for g in range(blocks // GROUP):
            lines = slice(g * GROUP * BLK, (g + 1) * GROUP * BLK)
            field = diffuse(1, h, g).astype(BF16)
            out[lines, columns] = (part[lines, columns] + dot(field, mix_wide[2])).astype(BF16)

    start_own(0, 0)
    stage(0, 1)
    start_own(0, 1)

    @pl.when(me == 0)
    def _():
        for p in range(2):
            for h in range(PARTS):
                halo[p, h, 0] = jnp.zeros((BLK, width), BF16)

    @pl.when(me == n - 1)
    def _():
        for p in range(2):
            for h in range(PARTS):
                halo[p, h, 1] = jnp.zeros((BLK, width), BF16)

    pass_z(0, 0)
    build()
    feat_copy.wait()
    pass_y(0, 0)
    pass_z(0, 1)
    finish(0, 0)
    hop_one(0)
    stage(1, 0)
    start_own(1, 0)
    pass_y(0, 1)
    pass_z(1, 0)
    finish(0, 1)
    hop_one(1)
    stage(1, 1)
    start_own(1, 1)
    mix_early(0)
    pass_y(1, 0)
    pass_z(1, 1)
    mix_early(1)
    finish(1, 0)
    hop_two(0)
    pass_y(1, 1)
    finish(1, 1)
    hop_two(1)
    for copy in sends:
        copy.wait_send()
    for p in range(2):
        for h in range(PARTS):

            @pl.when(me < n - 1)
            def _():
                halo_copy(p, h, 0, me + 1).wait_send()

            @pl.when(me > 0)
            def _():
                halo_copy(p, h, 1, me - 1).wait_send()


def hops(n, hidden, features, band, farw, mix, ptr, col, exports):
    rows, columns = hidden.shape
    ys = 2 if n == 16 else 1
    zs = n // (2 * ys)
    width = columns // PARTS
    chunk_sends = zs - 1 + (zs if ys > 1 else 0) + zs * ys
    vmem = pl.BlockSpec(memory_space=pltpu.VMEM)
    smem = pl.BlockSpec(memory_space=pltpu.SMEM)
    return pl.pallas_call(
        functools.partial(hops_kernel, n, zs, ys),
        in_specs=[vmem, pl.BlockSpec(memory_space=pl.ANY), vmem, vmem, vmem, smem, smem, smem],
        out_specs=vmem,
        out_shape=jax.ShapeDtypeStruct((rows, columns), BF16),
        scratch_shapes=[
            *[pltpu.VMEM((n * EXPORT, BLK, width), BF16)] * (2 * PARTS),
            pltpu.VMEM((2, PARTS, 2, BLK, width), BF16),
            pltpu.VMEM((2, PARTS, rows // BLK + 2, BLK, width), BF16),
            pltpu.VMEM((farw.shape[1], width), BF16),
            pltpu.VMEM((rows, farw.shape[1]), BF16),
            pltpu.VMEM((rows, (GROUP + 2) * BLK), BF16),
            pltpu.VMEM((3, width, width), BF16),
            pltpu.VMEM((rows, columns), BF16),
            pltpu.VMEM((rows, columns), F32),
            pltpu.SemaphoreType.DMA((2, PARTS, chunk_sends)),
            pltpu.SemaphoreType.DMA((2, PARTS, n)),
            pltpu.SemaphoreType.DMA((2, PARTS, 2)),
            pltpu.SemaphoreType.DMA((2, PARTS, 2)),
            pltpu.SemaphoreType.DMA((1,)),
        ],
        compiler_params=pltpu.CompilerParams(
            collective_id=0, has_side_effects=True, vmem_limit_bytes=60 * 2**20
        ),
        name="hops",
    )(hidden, features, band.T, farw, mix.T, ptr, col, exports.T)


def solution(mesh):
    n = mesh.shape["node"]

    def local(features, fg, skip, mix, band, farw, ptr, col, exports):
        hidden, skip_out = front(features, fg, skip)
        residual = hops(n, hidden, features, band, farw, mix, ptr, col, exports)
        return residual, skip_out

    rows = P(("groups", "node"), None)
    return jax.shard_map(
        local,
        mesh=mesh,
        in_specs=(
            rows, P(), P(), P(), P("node", None), P(None, "node"), P("node", None), P("node", None), P(),
        ),
        out_specs=(rows, rows),
        check_vma=False,
    )
```
